256 devices in a mesh: bulk: 16 (over z_hi, y, core), tensor: 16 (over z_lo, x).
Axes of the slice: x: 4, y: 4, z: 8 (z_hi: 2, z_lo: 4; z = z_hi * 4 + z_lo), core: 2. Of those that a mesh axis runs over, the one named last changes fastest.
Arguments:
- spectrum: bfloat16 [256, 2, 163840], P('tensor', None, 'bulk'), may hold values from -6 to 6
- out_grad: bfloat16 [256, 2, 163840], P('tensor', None, 'bulk'), may hold values from -6 to 6
- in_factor: bfloat16 [256, 1024], P(None, 'tensor'), may hold values from -0.375 to 0.375
- out_factor: bfloat16 [256, 1024], P(None, 'tensor'), may hold values from -0.375 to 0.375
- mode_factor: bfloat16 [1024, 2, 163840], P('tensor', None, 'bulk'), may hold values from -6 to 6
Outputs:
- grad_spectrum: bfloat16 [256, 2, 163840], P('tensor', None, 'bulk')
- grad_modes: bfloat16 [1024, 2, 163840], P('tensor', None, 'bulk')
- grad_in_factor: float32 [256, 1024], P(None, 'tensor')
- grad_out_factor: float32 [256, 1024], P(None, 'tensor')
The draws below stay inside these ranges and needn't reach their ends.
All inputs are finite; a program needn't handle non-finite values.
Results may differ from the reference program's by a relative error of at most 0.023.
Values may be sent and summed in bfloat16 or wider, within the bound.
No kernel may reach another device: no remote copies, remote signals or barrier semaphores. Data moves between devices by JAX's collectives and lax.ppermute only.
A program may use at most 128 MiB of HBM per device.

```python
import jax
import jax.numpy as jnp
from jax import lax

C = 256
R = 1024
MODES = 163840
N_TENSOR = 16


def steps_of(stream_key, extent, cuts, low, high):
    def one(position, shards_of):
        steps = jax.random.uniform(jax.random.fold_in(jax.random.fold_in(stream_key, 6), position), (shards_of,), jnp.float32, low / len(cuts), high / len(cuts))
        return jnp.repeat(jnp.exp(steps), extent[position] // shards_of).reshape((-1,) + (1,) * (len(extent) - position - 1))

    gain = one(*cuts[0])
    for cut in cuts[1:]:
        gain = gain * one(*cut)
    return gain


def bell_draw(own_key, dims, deviation, limit, cuts=(), kind=jnp.bfloat16):
    drawn = deviation * jax.random.normal(own_key, dims, jnp.float32)
    if cuts:
        drawn = drawn * steps_of(own_key, dims, cuts, -0.22, 0.18)
    return jnp.clip(drawn, -limit, limit).astype(kind)


def setup_inputs(seed: int = 0) -> dict:
    keys = jax.random.split(jax.random.key(seed), 6)
    spectrum = bell_draw(keys[0], (C, 2, MODES), 1.0, 6.0, ((0, 16), (2, 16)))
    out_grad = bell_draw(keys[1], (C, 2, MODES), 1.0, 6.0, ((0, 16), (2, 16)))
    in_factor = bell_draw(keys[2], (C, R), C ** -0.5, 0.375, ((1, 16),))
    out_factor = bell_draw(keys[3], (C, R), C ** -0.5, 0.375, ((1, 16),))
    mode_factor = bell_draw(keys[4], (R, 2, MODES), 1.0, 6.0, ((0, 16), (2, 16)))
    return dict(spectrum=spectrum, out_grad=out_grad, in_factor=in_factor, out_factor=out_factor, mode_factor=mode_factor)


def reference(spectrum, out_grad, in_factor, out_factor, mode_factor):
    scale = float(MODES) ** -0.5
    rank_dev = R // N_TENSOR
    in_slices = in_factor.reshape(C, N_TENSOR, rank_dev).transpose(1, 0, 2)
    out_slices = out_factor.reshape(C, N_TENSOR, rank_dev).transpose(1, 0, 2)
    mode_slices = mode_factor.reshape(N_TENSOR, rank_dev, 2, MODES)
    spec_f = spectrum.astype(jnp.float32)
    grad_f = out_grad.astype(jnp.float32)

    def slice_step(carry, pieces):
        in_part, out_part, mode_part = pieces
        in_f = in_part.astype(jnp.float32)
        out_f = out_part.astype(jnp.float32)
        mode_f = mode_part.astype(jnp.float32)
        u = jnp.einsum('cr,ctk->rtk', in_f, spec_f)
        v = jnp.einsum('or,otk->rtk', out_f, grad_f)
        m0, m1 = mode_f[:, 0], mode_f[:, 1]
        u0, u1 = u[:, 0], u[:, 1]
        v0, v1 = v[:, 0], v[:, 1]
        weighted = jnp.stack([m0 * u0 - m1 * u1, m0 * u1 + m1 * u0], axis=1).astype(jnp.bfloat16)
        pulled = jnp.stack([v0 * m0 + v1 * m1, v1 * m0 - v0 * m1], axis=1).astype(jnp.bfloat16)
        mode_grad = jnp.stack([v0 * u0 + v1 * u1, v1 * u0 - v0 * u1], axis=1).astype(jnp.bfloat16)
        pulled_f = pulled.astype(jnp.float32)
        weighted_f = weighted.astype(jnp.float32)
        partial_sum = jnp.einsum('cr,rtk->ctk', in_f, pulled_f).astype(jnp.bfloat16)
        partial_sum = lax.optimization_barrier(partial_sum)
        carry = carry + partial_sum.astype(jnp.float32)
        in_grad = scale * jnp.einsum('ctk,rtk->cr', spec_f, pulled_f)
        out_grad_part = scale * jnp.einsum('otk,rtk->or', grad_f, weighted_f)
        return carry, (mode_grad, in_grad, out_grad_part)

    start = jnp.zeros((C, 2, MODES), jnp.float32)
    total, (mode_grads, in_grads, out_grads) = lax.scan(slice_step, start, (in_slices, out_slices, mode_slices))
    grad_spectrum = total.astype(jnp.bfloat16)
    grad_modes = mode_grads.reshape(R, 2, MODES)
    grad_in_factor = in_grads.transpose(1, 0, 2).reshape(C, R)
    grad_out_factor = out_grads.transpose(1, 0, 2).reshape(C, R)
    return grad_spectrum, grad_modes, grad_in_factor, grad_out_factor
```

```python
import functools

import jax
import jax.numpy as jnp
from jax import lax
from jax.experimental import pallas as pl
from jax.experimental.pallas import tpu as pltpu
from jax.sharding import PartitionSpec as P

BF = jnp.bfloat16
F32 = jnp.float32
NX = 4
NZ = 4
ORDER = ((0, 1, 2, 3), (1, 0, 2, 3), (2, 3, 1, 0), (3, 2, 1, 0))


def x_shift(step):
    return [(z * NX + x, z * NX + (x + step) % NX) for z in range(NZ) for x in range(NX)]


def z_moves(pairs):
    return [(a * NX + x, b * NX + x) for a, b in pairs for x in range(NX)]


SWAP = z_moves([(0, 1), (1, 0), (2, 3), (3, 2)])
MIDDLE = z_moves([(1, 2), (2, 1)])
OUTWARD = z_moves([(1, 0), (2, 3)])
INWARD = z_moves([(0, 1), (3, 2)])


def send(a, moves):
    return lax.ppermute(a, "tensor", moves)


def send_bulk(a, move):
    return lax.ppermute(a, "bulk", [(i, move(i)) for i in range(16)])


def y_shift(step):
    return lambda i: (i // 8) * 8 + ((i // 2 % 4 + step) % 4) * 2 + i % 2


def nt_dot(a, b):
    return lax.dot_general(a, b, (((1,), (1,)), ((), ())), preferred_element_type=F32)


def nn_dot(a, b):
    return jnp.dot(a, b, preferred_element_type=F32)


def body(steps, info, *refs):
    spec, grad, mode, fac = refs[0:6], refs[6:12], refs[12:16], refs[16:20]
    gm, gs, d_in, d_out = refs[20:24], refs[24:28], refs[28], refs[29]
    f_in, ft_in, ft_out, tmp, acc_in, acc_out = refs[30:]
    k = pl.program_id(0)
    middle = info[16] == 1

    @pl.when(k == 0)
    def _():
        for which, rows, cols in ((0, f_in, ft_in), (1, None, ft_out)):
            whole = jnp.concatenate([f[which] for f in fac], axis=0).astype(F32)
            tmp[...] = whole.T
            for i in range(16):
                src = pl.ds(pl.multiple_of(info[i] * 16, 16), 16)
                acc_in[16 * i : 16 * i + 16, :] = tmp[src, :]
            if rows is not None:
                rows[...] = acc_in[...].astype(BF)
            cols[...] = acc_in[...].T.astype(BF)
        acc_in[...] = jnp.zeros_like(acc_in)
        acc_out[...] = jnp.zeros_like(acc_out)

    def gathered(parts, t):
        own, near, c_mid, c_end, d_mid, d_end = (p[t] for p in parts)
        return jnp.concatenate(
            [own, near, jnp.where(middle, c_mid, c_end), jnp.where(middle, d_mid, d_end)], axis=0
        )

    s = [gathered(spec, t) for t in range(2)]
    g = [gathered(grad, t) for t in range(2)]
    m0, m1 = [jnp.concatenate([m[t] for m in mode], axis=0).astype(F32) for t in range(2)]
    u0, u1 = [nn_dot(ft_in[...], a) for a in s]
    v0, v1 = [nn_dot(ft_out[...], a) for a in g]
    w = [(m0 * u0 - m1 * u1).astype(BF), (m0 * u1 + m1 * u0).astype(BF)]
    p = [(v0 * m0 + v1 * m1).astype(BF), (v1 * m0 - v0 * m1).astype(BF)]
    q = [(v0 * u0 + v1 * u1).astype(BF), (v1 * u0 - v0 * u1).astype(BF)]
    for t in range(2):
        part = nn_dot(f_in[...], p[t]).astype(BF)
        for i in range(4):
            gm[i][t] = q[t][64 * i : 64 * i + 64, :]
            gs[i][t] = part[64 * i : 64 * i + 64, :]
    acc_in[...] += nt_dot(s[0], p[0]) + nt_dot(s[1], p[1])
    acc_out[...] += nt_dot(g[0], w[0]) + nt_dot(g[1], w[1])

    @pl.when(k == steps - 1)
    def _():
        for acc, out in ((acc_in, d_in), (acc_out, d_out)):
            for i in range(16):
                dst = pl.ds(pl.multiple_of(info[i] * 16, 16), 16)
                tmp[dst, :] = acc[16 * i : 16 * i + 16, :]
            out[...] = tmp[...].T


def compute(info, spec, grad, mode, fac, tile=512):
    modes = mode[0].shape[2]
    steps = modes // tile
    block = (2, 64, tile)
    here = pl.BlockSpec(block, lambda k, n: (0, 0, k))
    mid = pl.BlockSpec(block, lambda k, n: (0, 0, k * n[16]))
    end = pl.BlockSpec(block, lambda k, n: (0, 0, k * (1 - n[16])))
    gathered = [here, here, mid, end, mid, end]
    whole = pl.BlockSpec((2, 64, 256), lambda k, n: (0, 0, 0))
    square = pl.BlockSpec((256, 256), lambda k, n: (0, 0))
    piece = jax.ShapeDtypeStruct((2, 64, modes), BF)
    factor = jax.ShapeDtypeStruct((256, 256), F32)
    outs = pl.pallas_call(
        functools.partial(body, steps),
        grid_spec=pltpu.PrefetchScalarGridSpec(
            num_scalar_prefetch=1,
            grid=(steps,),
            in_specs=gathered * 2 + [here] * 4 + [whole] * 4,
            out_specs=[here] * 8 + [square] * 2,
            scratch_shapes=[pltpu.VMEM((256, 256), BF)] * 3 + [pltpu.VMEM((256, 256), F32)] * 3,
        ),
        out_shape=[piece] * 8 + [factor] * 2,
        compiler_params=pltpu.CompilerParams(vmem_limit_bytes=40 * 1024 * 1024),
        cost_estimate=pl.CostEstimate(
            flops=20 * 256 * 256 * modes, bytes_accessed=10 * 256 * 2 * modes * 2, transcendentals=0
        ),
    )(info, *spec, *grad, *mode, *fac)
    return outs[0:4], outs[4:8], outs[8], outs[9]


def cut(a, x, d, size):
    start = ((x + d) % NX) * size
    return lax.dynamic_slice_in_dim(a, start, size, axis=2)


def scatter_x(a, x):
    size = a.shape[2] // NX
    parts = [cut(a, x, d, size) for d in range(NX)]
    return [parts[0]] + [send(parts[d], x_shift(d)) for d in range(1, NX)]


def collect_x(parts, x):
    size = parts[0].shape[2]
    parts = [parts[0]] + [send(parts[d], x_shift(-d)) for d in range(1, NX)]
    out = jnp.zeros(parts[0].shape[:2] + (size * NX,), BF)
    for d in range(NX):
        out = lax.dynamic_update_slice_in_dim(out, parts[d], ((x + d) % NX) * size, axis=2)
    return out


def gather_z(own):
    near = send(own, SWAP)
    c_mid = send(own, MIDDLE)
    d_mid = send(near, MIDDLE)
    c_end = send(c_mid, OUTWARD)
    d_end = send(d_mid, OUTWARD)
    return [own, near, c_mid, c_end, d_mid, d_end]


def add(a, b):
    return (a.astype(F32) + b.astype(F32)).astype(BF)


def scatter_z(own, near, c, d):
    d = add(d, send(d, INWARD))
    c = add(c, send(c, INWARD))
    near = add(near, send(d, MIDDLE))
    from_c = send(c, MIDDLE)
    from_near = send(near, SWAP)
    return (own.astype(F32) + from_c.astype(F32) + from_near.astype(F32)).astype(BF)


def on_device(spectrum, out_grad, in_factor, out_factor, mode_factor):
    scale = float(mode_factor.shape[2] * lax.axis_size("bulk")) ** (-0.5)
    place = lax.axis_index("tensor")
    x, z = place % NX, place // NX
    order = jnp.asarray(ORDER, jnp.int32)[z]
    blocks = order[:, None] * NX + (x - jnp.arange(NX, dtype=jnp.int32)[None, :]) % NX
    middle = ((z == 1) | (z == 2)).astype(jnp.int32)
    info = jnp.concatenate([blocks.reshape(16), middle[None]])

    turn = lambda a: jnp.transpose(a, (1, 0, 2))
    own_s = jnp.concatenate(scatter_x(turn(spectrum), x), axis=1)
    own_g = jnp.concatenate(scatter_x(turn(out_grad), x), axis=1)
    factors = jnp.stack([in_factor.T, out_factor.T])
    fac = [factors] + [send(factors, x_shift(d)) for d in range(1, NX)]
    spec = gather_z(own_s)
    grad = gather_z(own_g)
    mode_factor, _ = lax.optimization_barrier((mode_factor, own_g))
    mode = scatter_x(turn(mode_factor), x)

    gm, gs, d_in, d_out = compute(info, spec, grad, mode, fac)

    grad_spectrum = scatter_z(*gs)
    grad_modes = turn(collect_x(gm, x))
    grad_spectrum = collect_x([grad_spectrum[:, 16 * d : 16 * d + 16] for d in range(NX)], x)

    both = jnp.stack([d_in, d_out]).reshape(2, NX, 64, 256)
    total = both[:, 0]
    for d in range(1, NX):
        total = total + send(both[:, d], x_shift(-d))
    total = total + send_bulk(total, lambda i: i ^ 1)
    total = (total + send_bulk(total, y_shift(2))) + (
        send_bulk(total, y_shift(1)) + send_bulk(total, y_shift(3))
    )
    total = scale * (total + send_bulk(total, lambda i: i ^ 8))
    return (turn(grad_spectrum), grad_modes, total[0].T, total[1].T)


def solution(mesh):
    return jax.shard_map(
        on_device,
        mesh=mesh,
        in_specs=(
            P("tensor", None, "bulk"),
            P("tensor", None, "bulk"),
            P(None, "tensor"),
            P(None, "tensor"),
            P("tensor", None, "bulk"),
        ),
        out_specs=(
            P("tensor", None, "bulk"),
            P("tensor", None, "bulk"),
            P(None, "tensor"),
            P(None, "tensor"),
        ),
        check_vma=False,
    )
```

```python
import functools

import jax
import jax.numpy as jnp
from jax import lax
from jax.experimental import pallas as pl
from jax.experimental.pallas import tpu as pltpu
from jax.sharding import PartitionSpec as P

BF = jnp.bfloat16
F32 = jnp.float32
NX = 4
NZ = 4
ORDER = ((0, 1, 2, 3), (1, 0, 2, 3), (2, 3, 1, 0), (3, 2, 1, 0))


def x_shift(step):
    return [(z * NX + x, z * NX + (x + step) % NX) for z in range(NZ) for x in range(NX)]


def z_moves(pairs):
    return [(a * NX + x, b * NX + x) for a, b in pairs for x in range(NX)]


SWAP = z_moves([(0, 1), (1, 0), (2, 3), (3, 2)])
MIDDLE = z_moves([(1, 2), (2, 1)])
OUTWARD = z_moves([(1, 0), (2, 3)])
INWARD = z_moves([(0, 1), (3, 2)])


def send(a, moves):
    return lax.ppermute(a, "tensor", moves)


def send_bulk(a, move):
    return lax.ppermute(a, "bulk", [(i, move(i)) for i in range(16)])


def y_shift(step):
    return lambda i: (i // 8) * 8 + ((i // 2 % 4 + step) % 4) * 2 + i % 2


def nt_dot(a, b):
    return lax.dot_general(a, b, (((1,), (1,)), ((), ())), preferred_element_type=F32)


def nn_dot(a, b):
    return jnp.dot(a, b, preferred_element_type=F32)


TILE = 512
REST_TILE = 256
SHARE = 2048


def hbm(shape, kind):
    return pltpu.HBM(shape, kind)


def load_factors(pieces, info, tmp, acc, rows, cols_in, cols_out):
    for which, row, col in ((0, rows, cols_in), (1, None, cols_out)):
        tmp[...] = jnp.concatenate(pieces(which), axis=0).astype(F32).T
        for i in range(16):
            src = pl.ds(pl.multiple_of(info[i] * 16, 16), 16)
            acc[16 * i : 16 * i + 16, :] = tmp[src, :]
        if row is not None:
            row[...] = acc[...].astype(BF)
        col[...] = acc[...].T.astype(BF)


def store_factors(info, tmp, acc, out):
    for i in range(16):
        dst = pl.ds(pl.multiple_of(info[i] * 16, 16), 16)
        tmp[dst, :] = acc[16 * i : 16 * i + 16, :]
    out(tmp[...].T)


def products(s, g, mode, rows, cols_in, cols_out, acc_in, acc_out):
    m0, m1 = [a.astype(F32) for a in mode]
    u0, u1 = [nn_dot(cols_in[...], a) for a in s]
    v0, v1 = [nn_dot(cols_out[...], a) for a in g]
    w = [(m0 * u0 - m1 * u1).astype(BF), (m0 * u1 + m1 * u0).astype(BF)]
    p = [(v0 * m0 + v1 * m1).astype(BF), (v1 * m0 - v0 * m1).astype(BF)]
    q = [(v0 * u0 + v1 * u1).astype(BF), (v1 * u0 - v0 * u1).astype(BF)]
    acc_in[...] += nt_dot(s[0], p[0]) + nt_dot(s[1], p[1])
    acc_out[...] += nt_dot(g[0], w[0]) + nt_dot(g[1], w[1])
    return q, [nn_dot(rows[...], a) for a in p]


def shared_body(steps, at_middle, info, *refs):
    own, near, c, d = refs[0:4]
    mode, fac, old = refs[4:8], refs[8:12], refs[12 : -15]
    gm, gs, d_fac = refs[-15:-11], refs[-11:-7], refs[-7]
    rows, cols_in, cols_out, tmp, acc_in, acc_out = refs[-6:]
    k = pl.program_id(0)
    mine = info[16] == at_middle

    @pl.when(mine & (k == 0))
    def _():
        load_factors(lambda which: [f[which] for f in fac], info, tmp, acc_in, rows, cols_in, cols_out)
        acc_in[...] = jnp.zeros_like(acc_in)
        acc_out[...] = jnp.zeros_like(acc_out)

    if old:

        @pl.when(jnp.logical_not(mine) & (k == 0))
        def _():
            for src, dst in zip(old, (*gm, *gs, d_fac)):
                dst[...] = src[...]

    @pl.when(mine)
    def _():
        s, g = [
            [jnp.concatenate([own[t], near[t], c[t], d[t]], axis=0) for t in (base, base + 1)]
            for base in (0, 2)
        ]
        modes = [jnp.concatenate([m[t] for m in mode], axis=0) for t in range(2)]
        q, part = products(s, g, modes, rows, cols_in, cols_out, acc_in, acc_out)
        for t in range(2):
            whole = part[t].astype(BF)
            for i in range(4):
                gm[i][t] = q[t][64 * i : 64 * i + 64, :]
                gs[i][t] = whole[64 * i : 64 * i + 64, :]

    @pl.when(mine & (k == steps - 1))
    def _():
        for which, acc in ((0, acc_in), (1, acc_out)):

            def put(a):
                d_fac[which] = a

            store_factors(info, tmp, acc, put)


def shared(info, own, near, c, d, mode, at_middle, old=()):
    modes = own.shape[2]
    steps = modes // TILE

    def tiles(rows):
        return pl.BlockSpec((rows, 64, TILE), lambda k, n: (0, 0, jnp.where(n[16] == at_middle, k, 0)))

    last = mode[0].shape[2] // 256 - 1
    fac = pl.BlockSpec((2, 64, 256), lambda k, n: (0, 0, last))
    square = pl.BlockSpec((2, 256, 256), lambda k, n: (0, 0, 0))
    outs = pl.pallas_call(
        functools.partial(shared_body, steps, at_middle),
        grid_spec=pltpu.PrefetchScalarGridSpec(
            num_scalar_prefetch=1,
            grid=(steps,),
            in_specs=[tiles(4)] * 4
            + [tiles(2)] * 4
            + [fac] * 4
            + ([pl.BlockSpec((2, 64, TILE), lambda k, n: (0, 0, 0))] * 8 + [square] if old else []),
            out_specs=[tiles(2)] * 8 + [square],
            scratch_shapes=[pltpu.VMEM((256, 256), BF)] * 3 + [pltpu.VMEM((256, 256), F32)] * 3,
        ),
        out_shape=[hbm((2, 64, modes), BF)] * 8 + [hbm((2, 256, 256), F32)],
        input_output_aliases={13 + i: i for i in range(9)} if old else {},
        compiler_params=pltpu.CompilerParams(vmem_limit_bytes=32 * 1024 * 1024),
        cost_estimate=pl.CostEstimate(
            flops=20 * 256 * 256 * modes, bytes_accessed=10 * 256 * 2 * modes * 2, transcendentals=0
        ),
    )(info, own, near, c, d, *mode, *mode, *old)
    return list(outs)


def rest_body(steps, info, *refs):
    own, near, cd, mode, fac = refs[0], refs[1], refs[2], refs[3:7], refs[7:11]
    near_mode, near_fac = refs[11], refs[12]
    gm, gm_near, gs_own, gs_near, gs_cd, d_own = refs[13:17], *refs[17:22]
    scratch = refs[22:]
    weights = scratch[0:3], scratch[3:6]
    tmp, accs = scratch[6], (scratch[7:9], scratch[9:11])
    k = pl.program_id(0)
    middle = info[16] == 1
    here = pl.ds(pl.multiple_of(k * REST_TILE, REST_TILE), REST_TILE)

    @pl.when(middle & (k == 0))
    def _():
        load_factors(lambda which: [f[which] for f in fac], info, tmp, accs[0][0], *weights[0])
        load_factors(
            lambda which: [near_fac[2 * i + which] for i in range(4)], info, tmp, accs[0][0], *weights[1]
        )
        for pair in accs:
            for acc in pair:
                acc[...] = jnp.zeros_like(acc)

    @pl.when(middle)
    def _():
        s, g = [
            [jnp.concatenate([own[t], near[t], cd[t], cd[4 + t]], axis=0) for t in (base, base + 1)]
            for base in (0, 2)
        ]
        modes = (
            [jnp.concatenate([m[t] for m in mode], axis=0) for t in range(2)],
            [jnp.concatenate([near_mode[2 * i + t] for i in range(4)], axis=0) for t in range(2)],
        )
        q, part = products(s, g, modes[0], *weights[0], *accs[0])
        q_near, part_near = products(s, g, modes[1], *weights[1], *accs[1])
        for t in range(2):
            whole = (part[t] + part_near[t]).astype(BF)
            for i in range(4):
                gm[i][t] = q[t][64 * i : 64 * i + 64, :]
                gm_near[2 * i + t, :, here] = q_near[t][64 * i : 64 * i + 64, :]
            gs_own[t] = whole[0:64, :]
            gs_near[t] = whole[64:128, :]
            gs_cd[t] = whole[128:192, :]
            gs_cd[2 + t] = whole[192:256, :]

    @pl.when(middle & (k == steps - 1))
    def _():
        for which in range(2):

            def put_own(a):
                d_own[which] = a

            def put_near(a):
                for i in range(4):
                    gm_near[2 * i + which, :, steps * REST_TILE :] = a[64 * i : 64 * i + 64, :].astype(BF)

            store_factors(info, tmp, accs[0][which], put_own)
            store_factors(info, tmp, accs[1][which], put_near)


def rest(info, own, near, cd, mode, near_pay):
    modes = own.shape[2]
    steps = modes // REST_TILE
    first = (mode[0].shape[2] - 256 - modes) // REST_TILE

    def tiles(rows, base=0):
        return pl.BlockSpec((rows, 64, REST_TILE), lambda k, n: (0, 0, base + k * n[16]))

    def fixed(rows, at):
        return pl.BlockSpec((rows, 64, 256), lambda k, n: (0, 0, at))

    square = pl.BlockSpec((2, 256, 256), lambda k, n: (0, 0, 0))
    outs = pl.pallas_call(
        functools.partial(rest_body, steps),
        grid_spec=pltpu.PrefetchScalarGridSpec(
            num_scalar_prefetch=1,
            grid=(steps,),
            in_specs=[tiles(4), tiles(4), tiles(8)]
            + [tiles(2, first)] * 4
            + [fixed(2, mode[0].shape[2] // 256 - 1)] * 4
            + [tiles(8), fixed(8, modes // 256)],
            out_specs=[tiles(2)] * 4 + [pl.BlockSpec((8, 64, modes + 256), lambda k, n: (0, 0, 0)), tiles(2), tiles(2), tiles(4), square],
            scratch_shapes=[pltpu.VMEM((256, 256), BF)] * 6 + [pltpu.VMEM((256, 256), F32)] * 5,
        ),
        out_shape=[hbm((2, 64, modes), BF)] * 4
        + [hbm((8, 64, modes + 256), BF)]
        + [hbm((n, 64, modes), BF) for n in (2, 2, 4)]
        + [hbm((2, 256, 256), F32)],
        compiler_params=pltpu.CompilerParams(vmem_limit_bytes=40 * 1024 * 1024),
        cost_estimate=pl.CostEstimate(
            flops=40 * 256 * 256 * modes, bytes_accessed=16 * 256 * 2 * modes * 2, transcendentals=0
        ),
    )(info, own, near, cd, *mode, *mode, near_pay, near_pay)
    return list(outs[0:4]), *outs[4:]


def cut(a, x, d, size):
    return lax.dynamic_slice_in_dim(a, ((x + d) % NX) * size, size, axis=2)


def add(a, b):
    return (a.astype(F32) + b.astype(F32)).astype(BF)


def together(*arrays):
    return lax.optimization_barrier(arrays)


def on_device(spectrum, out_grad, in_factor, out_factor, mode_factor):
    scale = float(mode_factor.shape[2] * lax.axis_size("bulk")) ** (-0.5)
    size = mode_factor.shape[2] // NX
    share = SHARE
    place = lax.axis_index("tensor")
    x, z = place % NX, place // NX
    order = jnp.asarray(ORDER, jnp.int32)[z]
    blocks = order[:, None] * NX + (x - jnp.arange(NX, dtype=jnp.int32)[None, :]) % NX
    middle = (z == 1) | (z == 2)
    info = jnp.concatenate([blocks.reshape(16), middle.astype(jnp.int32)[None]])
    turn = lambda a: jnp.transpose(a, (1, 0, 2))

    both = jnp.concatenate([turn(spectrum), turn(out_grad)], axis=0)
    parts = [cut(both, x, d, size) for d in range(NX)]
    parts = [parts[0]] + [send(parts[d], x_shift(d)) for d in range(1, NX)]
    own_a = jnp.concatenate([a[:, :, :share] for a in parts], axis=1)
    own_b = jnp.concatenate([a[:, :, share:] for a in parts], axis=1)

    factors = jnp.stack([in_factor.T, out_factor.T])
    turned = turn(mode_factor)
    mode = [jnp.concatenate([cut(turned, x, d, size), factors], axis=2) for d in range(NX)]

    own_a, mode = together(own_a, mode)
    near_a, c_mid = send(own_a, SWAP), send(own_a, MIDDLE)
    mode[1], mode[3] = send(mode[1], x_shift(1)), send(mode[3], x_shift(3))
    near_a, c_mid, own_b, mode = together(near_a, c_mid, own_b, mode)
    d_mid, c_end, near_b = send(near_a, MIDDLE), send(c_mid, OUTWARD), send(own_b, INWARD)
    mode[2] = send(mode[2], x_shift(2))
    d_mid, c_end, near_b, mode = together(d_mid, c_end, near_b, mode)
    d_end = send(d_mid, OUTWARD)
    near_pay = send(jnp.concatenate([a[:, :, share:] for a in mode], axis=0), INWARD)
    cd_b = send(jnp.concatenate([own_b, near_b], axis=0), MIDDLE)
    old = shared(info, own_a, near_a, c_mid, d_mid, mode, 1)
    near_pay, cd_b, d_end, old = together(near_pay, cd_b, d_end, old)

    gm_b, gm_near, gs_own, gs_near, gs_cd, d_own = rest(info, own_b, near_b, cd_b, mode, near_pay)
    gm_near, own_a = together(gm_near, own_a)
    pay = send(gm_near, OUTWARD)
    outs = shared(info, own_a, near_a, c_end, d_end, mode, 0, old)
    gm_a, (own, near, c, d), d_fac = outs[0:4], outs[4:8], outs[8]

    d, gm_a = together(d, gm_a)
    from_d = send(d, INWARD)
    gm_a[1], gm_a[3] = send(gm_a[1], x_shift(-1)), send(gm_a[3], x_shift(-3))
    from_d, pay, c, gm_a = together(from_d, pay, c, gm_a)
    from_c = send(c, INWARD)
    d = send(jnp.concatenate([add(d, from_d), gs_cd[2:4]], axis=2), MIDDLE)
    fac = d_fac.reshape(2, NX, 64, 256)
    own_fac = d_own.reshape(2, NX, 64, 256)
    gm_b = [
        jnp.where(
            middle,
            jnp.concatenate([gm_b[i], (fac[:, i] + own_fac[:, i]).astype(BF)], axis=2),
            jnp.concatenate(
                [pay[2 * i : 2 * i + 2, :, :-256], (fac[:, i] + pay[2 * i : 2 * i + 2, :, -256:]).astype(BF)], axis=2
            ),
        )
        for i in range(NX)
    ]
    gm_b = [gm_b[0]] + [send(gm_b[i], x_shift(-i)) for i in range(1, NX)]
    from_c, d, gm_b, gm_a = together(from_c, d, gm_b, gm_a)
    zero = jnp.zeros_like(gs_own)
    near = add(jnp.concatenate([near, jnp.where(middle, gs_near, zero)], axis=2), d)
    c = send(jnp.concatenate([add(c, from_c), gs_cd[0:2]], axis=2), MIDDLE)
    near = send(near, SWAP)
    gm_a[2] = send(gm_a[2], x_shift(2))
    fac = [a[:, :, -256:].astype(F32) for a in gm_b]
    total = (fac[0] + fac[1]) + (fac[2] + fac[3])
    core = lax.axis_index("bulk") % 2
    mine, other = jnp.where(core == 0, total, total[::-1])
    mine = mine + send_bulk(other, lambda i: i ^ 1)
    mine = mine + send_bulk(mine, lambda i: i ^ 4)
    mine = mine + send_bulk(mine, lambda i: i ^ 2)
    c, near, gm_a, mine = together(c, near, gm_a, mine)
    own = jnp.concatenate([own, jnp.where(middle, gs_own, zero)], axis=2).astype(F32)
    own = (own + c.astype(F32) + near.astype(F32)).astype(BF)
    own = [own[:, 16 * i : 16 * i + 16] for i in range(NX)]
    own = [own[0]] + [send(own[i], x_shift(-i)) for i in range(1, NX)]
    mine = scale * (mine + send_bulk(mine, lambda i: i ^ 8))
    other = send_bulk(mine, lambda i: i ^ 1)
    grad_in = jnp.where(core == 0, mine, other)
    grad_out = jnp.where(core == 0, other, mine)

    def join(parts):
        out = jnp.zeros(parts[0].shape[:2] + (size * NX,), BF)
        for d in range(NX):
            out = lax.dynamic_update_slice_in_dim(out, parts[d], ((x + d) % NX) * size, axis=2)
        return turn(out)

    grad_modes = join([jnp.concatenate([a, b[:, :, :-256]], axis=2) for a, b in zip(gm_a, gm_b)])
    return (join(own), grad_modes, grad_in.T, grad_out.T)


def solution(mesh):
    return jax.shard_map(
        on_device,
        mesh=mesh,
        in_specs=(
            P("tensor", None, "bulk"),
            P("tensor", None, "bulk"),
            P(None, "tensor"),
            P(None, "tensor"),
            P("tensor", None, "bulk"),
        ),
        out_specs=(
            P("tensor", None, "bulk"),
            P("tensor", None, "bulk"),
            P(None, "tensor"),
            P(None, "tensor"),
        ),
        check_vma=False,
    )
```

```python
import functools

import jax
import jax.numpy as jnp
from jax import lax
from jax.experimental import pallas as pl
from jax.experimental.pallas import tpu as pltpu
from jax.sharding import PartitionSpec as P

BF = jnp.bfloat16
F32 = jnp.float32
NX = 4
NZ = 4
ORDER = ((0, 1, 2, 3), (1, 0, 2, 3), (2, 3, 1, 0), (3, 2, 1, 0))


def x_shift(step):
    return [(z * NX + x, z * NX + (x + step) % NX) for z in range(NZ) for x in range(NX)]


def z_moves(pairs):
    return [(a * NX + x, b * NX + x) for a, b in pairs for x in range(NX)]


SWAP = z_moves([(0, 1), (1, 0), (2, 3), (3, 2)])
MIDDLE = z_moves([(1, 2), (2, 1)])
OUTWARD = z_moves([(1, 0), (2, 3)])
INWARD = z_moves([(0, 1), (3, 2)])


def send(a, moves):
    return lax.ppermute(a, "tensor", moves)


def send_bulk(a, move):
    return lax.ppermute(a, "bulk", [(i, move(i)) for i in range(16)])


def y_shift(step):
    return lambda i: (i // 8) * 8 + ((i // 2 % 4 + step) % 4) * 2 + i % 2


def nt_dot(a, b):
    return lax.dot_general(a, b, (((1,), (1,)), ((), ())), preferred_element_type=F32)


def nn_dot(a, b):
    return jnp.dot(a, b, preferred_element_type=F32)


TILE = 256
SHARE = 1792


def hbm(shape, kind):
    return pltpu.HBM(shape, kind)


def load_factors(pieces, info, tmp, acc, rows, cols_in, cols_out):
    for which, row, col in ((0, rows, cols_in), (1, None, cols_out)):
        tmp[...] = jnp.concatenate(pieces(which), axis=0).astype(F32).T
        for i in range(16):
            src = pl.ds(pl.multiple_of(info[i] * 16, 16), 16)
            acc[16 * i : 16 * i + 16, :] = tmp[src, :]
        if row is not None:
            row[...] = acc[...].astype(BF)
        col[...] = acc[...].T.astype(BF)


def store_factors(info, tmp, acc, out):
    for i in range(16):
        dst = pl.ds(pl.multiple_of(info[i] * 16, 16), 16)
        tmp[dst, :] = acc[16 * i : 16 * i + 16, :]
    out(tmp[...].T)


def products(s, g, mode, rows, cols_in, cols_out, acc_in, acc_out):
    m0, m1 = [a.astype(F32) for a in mode]
    u0, u1 = [nn_dot(cols_in[...], a) for a in s]
    v0, v1 = [nn_dot(cols_out[...], a) for a in g]
    w = [(m0 * u0 - m1 * u1).astype(BF), (m0 * u1 + m1 * u0).astype(BF)]
    p = [(v0 * m0 + v1 * m1).astype(BF), (v1 * m0 - v0 * m1).astype(BF)]
    q = [(v0 * u0 + v1 * u1).astype(BF), (v1 * u0 - v0 * u1).astype(BF)]
    acc_in[...] += nt_dot(s[0], p[0]) + nt_dot(s[1], p[1])
    acc_out[...] += nt_dot(g[0], w[0]) + nt_dot(g[1], w[1])
    return q, [nn_dot(rows[...], a) for a in p]


def share_step(own, near, c, d, mode, weights, accs, gm, gs):
    s, g = [
        [jnp.concatenate([own[t], near[t], c[t], d[t]], axis=0) for t in (base, base + 1)]
        for base in (0, 2)
    ]
    modes = [jnp.concatenate([m[t] for m in mode], axis=0) for t in range(2)]
    q, part = products(s, g, modes, *weights, *accs)
    for t in range(2):
        whole = part[t].astype(BF)
        for i in range(4):
            gm[i][t] = q[t][64 * i : 64 * i + 64, :]
            gs[i][t] = whole[64 * i : 64 * i + 64, :]


def shared_body(steps, info, *refs):
    own, near, c, d = refs[0:4]
    mode, fac = refs[4:8], refs[8:12]
    gm, gs, d_fac = refs[12:16], refs[16:20], refs[20]
    weights, tmp, accs = refs[21:24], refs[24], refs[25:27]
    k = pl.program_id(0)
    middle = info[16] == 1

    @pl.when(middle & (k == 0))
    def _():
        load_factors(lambda which: [f[which] for f in fac], info, tmp, accs[0], *weights)
        for acc in accs:
            acc[...] = jnp.zeros_like(acc)

    @pl.when(middle)
    def _():
        share_step(own, near, c, d, mode, weights, accs, gm, gs)

    @pl.when(middle & (k == steps - 1))
    def _():
        for which, acc in enumerate(accs):

            def put(a):
                d_fac[which] = a

            store_factors(info, tmp, acc, put)


def shared_middle(info, own, near, c, d, mode):
    modes = own.shape[2]
    steps = modes // TILE

    def tiles(rows):
        return pl.BlockSpec((rows, 64, TILE), lambda k, n: (0, 0, k * n[16]))

    last = mode[0].shape[2] // 256 - 1
    fac = pl.BlockSpec((2, 64, 256), lambda k, n: (0, 0, last))
    square = pl.BlockSpec((2, 256, 256), lambda k, n: (0, 0, 0))
    return pl.pallas_call(
        functools.partial(shared_body, steps),
        grid_spec=pltpu.PrefetchScalarGridSpec(
            num_scalar_prefetch=1,
            grid=(steps,),
            in_specs=[tiles(4)] * 4 + [tiles(2)] * 4 + [fac] * 4,
            out_specs=[tiles(2)] * 8 + [square],
            scratch_shapes=[pltpu.VMEM((256, 256), BF)] * 3 + [pltpu.VMEM((256, 256), F32)] * 3,
        ),
        out_shape=[hbm((2, 64, modes), BF)] * 8 + [hbm((2, 256, 256), F32)],
        compiler_params=pltpu.CompilerParams(vmem_limit_bytes=32 * 1024 * 1024),
        cost_estimate=pl.CostEstimate(
            flops=20 * 256 * 256 * modes, bytes_accessed=10 * 256 * 2 * modes * 2, transcendentals=0
        ),
    )(info, own, near, c, d, *mode, *mode)


def last_body(steps, info, *refs):
    own, near, c, d = refs[0:4]
    mode, fac, old = refs[4:8], refs[8:12], refs[12:20]
    own_b, near_b, cd, near_mode, near_fac = refs[20:25]
    gm, gs, d_fac = refs[25:29], refs[29:33], refs[33]
    gm_b, pay, gs_own, gs_near, gs_cd = refs[34:38], *refs[38:42]
    weights, near_weights, tmp = refs[42:45], refs[45:48], refs[48]
    accs, near_accs = refs[49:51], refs[51:53]
    k = pl.program_id(0)
    middle = info[16] == 1
    rest = pay.shape[2] - 256

    @pl.when(k == 0)
    def _():
        load_factors(lambda which: [f[which] for f in fac], info, tmp, accs[0], *weights)
        for acc in accs:
            acc[...] = jnp.zeros_like(acc)

    @pl.when(middle & (k == 0))
    def _():
        load_factors(
            lambda which: [near_fac[2 * i + which] for i in range(4)], info, tmp, near_accs[0], *near_weights
        )
        for acc in near_accs:
            acc[...] = jnp.zeros_like(acc)
        for src, dst in zip(old, (*gm, *gs)):
            dst[...] = src[...]

    @pl.when(jnp.logical_not(middle))
    def _():
        share_step(own, near, c, d, mode, weights, accs, gm, gs)

    @pl.when(middle & (k < rest // TILE))
    def _():
        s, g = [
            [jnp.concatenate([own_b[t], near_b[t], cd[t], cd[4 + t]], axis=0) for t in (base, base + 1)]
            for base in (0, 2)
        ]
        modes = [jnp.concatenate([m[t] for m in mode], axis=0) for t in range(2)]
        near_modes = [jnp.concatenate([near_mode[2 * i + t] for i in range(4)], axis=0) for t in range(2)]
        q, part = products(s, g, modes, *weights, *accs)
        q_near, part_near = products(s, g, near_modes, *near_weights, *near_accs)
        here = pl.ds(pl.multiple_of(k * TILE, TILE), TILE)
        for t in range(2):
            whole = (part[t] + part_near[t]).astype(BF)
            for i in range(4):
                gm_b[i][t] = q[t][64 * i : 64 * i + 64, :]
                pay[2 * i + t, :, here] = q_near[t][64 * i : 64 * i + 64, :]
            gs_own[t] = whole[0:64, :]
            gs_near[t] = whole[64:128, :]
            gs_cd[t] = whole[128:192, :]
            gs_cd[2 + t] = whole[192:256, :]

    @pl.when(middle & (k == rest // TILE - 1))
    def _():
        for which, acc in enumerate(near_accs):

            def put(a):
                for i in range(4):
                    pay[2 * i + which, :, rest:] = a[64 * i : 64 * i + 64, :].astype(BF)

            store_factors(info, tmp, acc, put)

    @pl.when(k == steps - 1)
    def _():
        for which, acc in enumerate(accs):

            def put(a):
                d_fac[which] = a

            store_factors(info, tmp, acc, put)


def last(info, own, near, c, d, mode, old, own_b, near_b, cd, near_pay):
    modes, rest = own.shape[2], own_b.shape[2]
    steps, rest_steps = modes // TILE, rest // TILE

    def ends(rows):
        return pl.BlockSpec((rows, 64, TILE), lambda k, n: (0, 0, k * (1 - n[16])))

    def middles(rows):
        return pl.BlockSpec((rows, 64, TILE), lambda k, n: (0, 0, jnp.minimum(k, rest_steps - 1) * n[16]))

    def fixed(rows, at):
        return pl.BlockSpec((rows, 64, 256), lambda k, n: (0, 0, at))

    both = pl.BlockSpec(
        (2, 64, TILE),
        lambda k, n: (0, 0, jnp.where(n[16] == 1, steps + jnp.minimum(k, rest_steps - 1), k)),
    )
    square = pl.BlockSpec((2, 256, 256), lambda k, n: (0, 0, 0))
    outs = pl.pallas_call(
        functools.partial(last_body, steps),
        grid_spec=pltpu.PrefetchScalarGridSpec(
            num_scalar_prefetch=1,
            grid=(steps,),
            in_specs=[ends(4)] * 4
            + [both] * 4
            + [fixed(2, mode[0].shape[2] // 256 - 1)] * 4
            + [fixed(2, 0)] * 8
            + [middles(4), middles(4), middles(8), middles(8), fixed(8, rest // 256)],
            out_specs=[ends(2)] * 8
            + [square]
            + [middles(2)] * 4
            + [pl.BlockSpec((8, 64, rest + 256), lambda k, n: (0, 0, 0))]
            + [middles(2), middles(2), middles(4)],
            scratch_shapes=[pltpu.VMEM((256, 256), BF)] * 6 + [pltpu.VMEM((256, 256), F32)] * 5,
        ),
        out_shape=[hbm((2, 64, modes), BF)] * 8
        + [hbm((2, 256, 256), F32)]
        + [hbm((2, 64, rest), BF)] * 4
        + [hbm((8, 64, rest + 256), BF)]
        + [hbm((n, 64, rest), BF) for n in (2, 2, 4)],
        input_output_aliases={13 + i: i for i in range(8)},
        compiler_params=pltpu.CompilerParams(vmem_limit_bytes=40 * 1024 * 1024),
        cost_estimate=pl.CostEstimate(
            flops=20 * 256 * 256 * modes, bytes_accessed=10 * 256 * 2 * modes * 2, transcendentals=0
        ),
    )(info, own, near, c, d, *mode, *mode, *old, own_b, near_b, cd, near_pay, near_pay)
    return list(outs[0:4]), outs[4:8], outs[8], list(outs[9:13]), *outs[13:]


def cut(a, x, d, size):
    return lax.dynamic_slice_in_dim(a, ((x + d) % NX) * size, size, axis=2)


def add(a, b):
    return (a.astype(F32) + b.astype(F32)).astype(BF)


def together(*arrays):
    return lax.optimization_barrier(arrays)


def on_device(spectrum, out_grad, in_factor, out_factor, mode_factor):
    scale = float(mode_factor.shape[2] * lax.axis_size("bulk")) ** (-0.5)
    size = mode_factor.shape[2] // NX
    share = SHARE
    place = lax.axis_index("tensor")
    x, z = place % NX, place // NX
    order = jnp.asarray(ORDER, jnp.int32)[z]
    blocks = order[:, None] * NX + (x - jnp.arange(NX, dtype=jnp.int32)[None, :]) % NX
    middle = (z == 1) | (z == 2)
    info = jnp.concatenate([blocks.reshape(16), middle.astype(jnp.int32)[None]])
    turn = lambda a: jnp.transpose(a, (1, 0, 2))

    both = jnp.concatenate([turn(spectrum), turn(out_grad)], axis=0)
    parts = [cut(both, x, d, size) for d in range(NX)]
    parts = [parts[0]] + [send(parts[d], x_shift(d)) for d in range(1, NX)]
    own_a = jnp.concatenate([a[:, :, :share] for a in parts], axis=1)
    own_b = jnp.concatenate([a[:, :, share:] for a in parts], axis=1)

    factors = jnp.stack([in_factor.T, out_factor.T])
    turned = turn(mode_factor)
    mode = [jnp.concatenate([cut(turned, x, d, size), factors], axis=2) for d in range(NX)]

    own_a, mode = together(own_a, mode)
    near_a, c_mid = send(own_a, SWAP), send(own_a, MIDDLE)
    mode = [mode[0]] + [send(mode[i], x_shift(i)) for i in range(1, NX)]
    near_a, c_mid, own_b = together(near_a, c_mid, own_b)
    d_mid, c_end, near_b = send(near_a, MIDDLE), send(c_mid, OUTWARD), send(own_b, INWARD)
    d_mid, c_end, near_b = together(d_mid, c_end, near_b)
    d_end = send(d_mid, OUTWARD)
    near_pay = send(jnp.concatenate([a[:, :, share:] for a in mode], axis=0), INWARD)
    cd_b = send(jnp.concatenate([own_b, near_b], axis=0), MIDDLE)
    *old, d_mid_fac = shared_middle(info, own_a, near_a, c_mid, d_mid, mode)
    near_pay, cd_b, d_end, old, d_mid_fac = together(near_pay, cd_b, d_end, old, d_mid_fac)
    gm_a, (own, near, c, d), d_fac, gm_b, pay, gs_own, gs_near, gs_cd = last(
        info, own_a, near_a, c_end, d_end, mode, old, own_b, near_b, cd_b, near_pay
    )

    from_d = send(d, INWARD)
    pay = send(pay, OUTWARD)
    gm_a[1], gm_a[3] = send(gm_a[1], x_shift(-1)), send(gm_a[3], x_shift(-3))
    from_d, c = together(from_d, c)
    from_c = send(c, INWARD)
    d = send(jnp.concatenate([add(d, from_d), gs_cd[2:4]], axis=2), MIDDLE)
    fac = d_fac.reshape(2, NX, 64, 256)
    mid_fac = d_mid_fac.reshape(2, NX, 64, 256)
    gm_b = [
        jnp.where(
            middle,
            jnp.concatenate([gm_b[i], (fac[:, i] + mid_fac[:, i]).astype(BF)], axis=2),
            jnp.concatenate(
                [pay[2 * i : 2 * i + 2, :, :-256], (fac[:, i] + pay[2 * i : 2 * i + 2, :, -256:]).astype(BF)], axis=2
            ),
        )
        for i in range(NX)
    ]
    gm_b = [gm_b[0]] + [send(gm_b[i], x_shift(-i)) for i in range(1, NX)]
    from_c, d, gm_a = together(from_c, d, gm_a)
    zero = jnp.zeros_like(gs_own)
    near = add(jnp.concatenate([near, jnp.where(middle, gs_near, zero)], axis=2), d)
    c = send(jnp.concatenate([add(c, from_c), gs_cd[0:2]], axis=2), MIDDLE)
    near = send(near, SWAP)
    gm_a[2] = send(gm_a[2], x_shift(2))
    fac = [a[:, :, -256:].astype(F32) for a in gm_b]
    total = (fac[0] + fac[1]) + (fac[2] + fac[3])
    core = lax.axis_index("bulk") % 2
    mine, other = jnp.where(core == 0, total, total[::-1])
    mine = mine + send_bulk(other, lambda i: i ^ 1)
    mine = mine + send_bulk(mine, lambda i: i ^ 4)
    mine = mine + send_bulk(mine, lambda i: i ^ 2)
    mine = mine + send_bulk(mine, lambda i: i ^ 8)
    c, near, gm_a, gm_b, mine = together(c, near, gm_a, gm_b, mine)
    own = jnp.concatenate([own, jnp.where(middle, gs_own, zero)], axis=2).astype(F32)
    own = (own + c.astype(F32) + near.astype(F32)).astype(BF)
    own = [own[:, 16 * i : 16 * i + 16] for i in range(NX)]
    own = [own[0]] + [send(own[i], x_shift(-i)) for i in range(1, NX)]
    mine = scale * mine
    other = send_bulk(mine, lambda i: i ^ 1)
    grad_in = jnp.where(core == 0, mine, other)
    grad_out = jnp.where(core == 0, other, mine)

    def join(parts):
        out = jnp.zeros(parts[0].shape[:2] + (size * NX,), BF)
        for d in range(NX):
            out = lax.dynamic_update_slice_in_dim(out, parts[d], ((x + d) % NX) * size, axis=2)
        return turn(out)

    grad_modes = join([jnp.concatenate([a, b[:, :, :-256]], axis=2) for a, b in zip(gm_a, gm_b)])
    return (join(own), grad_modes, grad_in.T, grad_out.T)


def solution(mesh):
    return jax.shard_map(
        on_device,
        mesh=mesh,
        in_specs=(
            P("tensor", None, "bulk"),
            P("tensor", None, "bulk"),
            P(None, "tensor"),
            P(None, "tensor"),
            P("tensor", None, "bulk"),
        ),
        out_specs=(
            P("tensor", None, "bulk"),
            P("tensor", None, "bulk"),
            P(None, "tensor"),
            P(None, "tensor"),
        ),
        check_vma=False,
    )
```

```python
import functools

import jax
import jax.numpy as jnp
from jax import lax
from jax.experimental import pallas as pl
from jax.experimental.pallas import tpu as pltpu
from jax.sharding import PartitionSpec as P

BF = jnp.bfloat16
F32 = jnp.float32
NX = 4
NZ = 4
ORDER = ((0, 1, 2, 3), (1, 0, 2, 3), (2, 3, 1, 0), (3, 2, 1, 0))


def x_shift(step):
    return [(z * NX + x, z * NX + (x + step) % NX) for z in range(NZ) for x in range(NX)]


def z_moves(pairs):
    return [(a * NX + x, b * NX + x) for a, b in pairs for x in range(NX)]


SWAP = z_moves([(0, 1), (1, 0), (2, 3), (3, 2)])
MIDDLE = z_moves([(1, 2), (2, 1)])
OUTWARD = z_moves([(1, 0), (2, 3)])
INWARD = z_moves([(0, 1), (3, 2)])


def send(a, moves):
    return lax.ppermute(a, "tensor", moves)


def send_bulk(a, move):
    return lax.ppermute(a, "bulk", [(i, move(i)) for i in range(16)])


def y_shift(step):
    return lambda i: (i // 8) * 8 + ((i // 2 % 4 + step) % 4) * 2 + i % 2


def nt_dot(a, b):
    return lax.dot_general(a, b, (((1,), (1,)), ((), ())), preferred_element_type=F32)


def nn_dot(a, b):
    return jnp.dot(a, b, preferred_element_type=F32)


TILE = 896
SHARE = 1792


def hbm(shape, kind):
    return pltpu.HBM(shape, kind)


def load_factors(pieces, info, tmp, acc, rows, cols_in, cols_out):
    for which, row, col in ((0, rows, cols_in), (1, None, cols_out)):
        tmp[...] = jnp.concatenate(pieces(which), axis=0).astype(F32).T
        for i in range(16):
            src = pl.ds(pl.multiple_of(info[i] * 16, 16), 16)
            acc[16 * i : 16 * i + 16, :] = tmp[src, :]
        if row is not None:
            row[...] = acc[...].astype(BF)
        col[...] = acc[...].T.astype(BF)


def store_factors(info, tmp, acc, out):
    for i in range(16):
        dst = pl.ds(pl.multiple_of(info[i] * 16, 16), 16)
        tmp[dst, :] = acc[16 * i : 16 * i + 16, :]
    out(tmp[...].T)


def products(s, g, mode, rows, cols_in, cols_out, acc_in, acc_out):
    m0, m1 = [a.astype(F32) for a in mode]
    u0, u1 = [nn_dot(cols_in[...], a) for a in s]
    v0, v1 = [nn_dot(cols_out[...], a) for a in g]
    w = [(m0 * u0 - m1 * u1).astype(BF), (m0 * u1 + m1 * u0).astype(BF)]
    p = [(v0 * m0 + v1 * m1).astype(BF), (v1 * m0 - v0 * m1).astype(BF)]
    q = [(v0 * u0 + v1 * u1).astype(BF), (v1 * u0 - v0 * u1).astype(BF)]
    acc_in[...] += nt_dot(s[0], p[0]) + nt_dot(s[1], p[1])
    acc_out[...] += nt_dot(g[0], w[0]) + nt_dot(g[1], w[1])
    return q, [nn_dot(rows[...], a) for a in p]


def share_step(own, near, c, d, mode, weights, accs, gm, gs):
    s, g = [
        [jnp.concatenate([own[t], near[t], c[t], d[t]], axis=0) for t in (base, base + 1)]
        for base in (0, 2)
    ]
    modes = [jnp.concatenate([m[t] for m in mode], axis=0) for t in range(2)]
    q, part = products(s, g, modes, *weights, *accs)
    for t in range(2):
        whole = part[t].astype(BF)
        for i in range(4):
            gm[i][t] = q[t][64 * i : 64 * i + 64, :]
            gs[i][t] = whole[64 * i : 64 * i + 64, :]


def shared_body(steps, info, *refs):
    own, near, c, d = refs[0:4]
    mode, fac = refs[4:8], refs[8:12]
    gm, gs, d_fac = refs[12:16], refs[16:20], refs[20]
    weights, tmp, accs = refs[21:24], refs[24], refs[25:27]
    k = pl.program_id(0)
    middle = info[16] == 1

    @pl.when(middle & (k == 0))
    def _():
        load_factors(lambda which: [f[which] for f in fac], info, tmp, accs[0], *weights)
        for acc in accs:
            acc[...] = jnp.zeros_like(acc)

    @pl.when(middle)
    def _():
        share_step(own, near, c, d, mode, weights, accs, gm, gs)

    @pl.when(middle & (k == steps - 1))
    def _():
        for which, acc in enumerate(accs):

            def put(a):
                d_fac[which] = a

            store_factors(info, tmp, acc, put)


def shared_middle(info, own, near, c, d, mode):
    modes = own.shape[2]
    steps = modes // TILE

    def tiles(rows):
        return pl.BlockSpec((rows, 64, TILE), lambda k, n: (0, 0, k * n[16]))

    last = mode[0].shape[2] // 256 - 1
    fac = pl.BlockSpec((2, 64, 256), lambda k, n: (0, 0, last))
    square = pl.BlockSpec((2, 256, 256), lambda k, n: (0, 0, 0))
    return pl.pallas_call(
        functools.partial(shared_body, steps),
        grid_spec=pltpu.PrefetchScalarGridSpec(
            num_scalar_prefetch=1,
            grid=(steps,),
            in_specs=[tiles(4)] * 4 + [tiles(2)] * 4 + [fac] * 4,
            out_specs=[tiles(2)] * 8 + [square],
            scratch_shapes=[pltpu.VMEM((256, 256), BF)] * 3 + [pltpu.VMEM((256, 256), F32)] * 3,
        ),
        out_shape=[hbm((2, 64, modes), BF)] * 8 + [hbm((2, 256, 256), F32)],
        compiler_params=pltpu.CompilerParams(vmem_limit_bytes=36 * 1024 * 1024),
        cost_estimate=pl.CostEstimate(
            flops=20 * 256 * 256 * modes, bytes_accessed=10 * 256 * 2 * modes * 2, transcendentals=0
        ),
    )(info, own, near, c, d, *mode, *mode)


def last_body(steps, info, *refs):
    own, near, c, d = refs[0:4]
    mode, fac, old = refs[4:8], refs[8:12], refs[12:20]
    own_b, near_b, cd, near_mode, near_fac = refs[20:25]
    gm, gs, d_fac = refs[25:29], refs[29:33], refs[33]
    gm_b, pay, gs_own, gs_near, gs_cd = refs[34:38], *refs[38:42]
    weights, near_weights, tmp = refs[42:45], refs[45:48], refs[48]
    accs, near_accs = refs[49:51], refs[51:53]
    k = pl.program_id(0)
    middle = info[16] == 1
    rest = pay.shape[2] - 256

    @pl.when(k == 0)
    def _():
        load_factors(lambda which: [f[which] for f in fac], info, tmp, accs[0], *weights)
        for acc in accs:
            acc[...] = jnp.zeros_like(acc)

    @pl.when(middle & (k == 0))
    def _():
        load_factors(
            lambda which: [near_fac[2 * i + which] for i in range(4)], info, tmp, near_accs[0], *near_weights
        )
        for acc in near_accs:
            acc[...] = jnp.zeros_like(acc)
        for src, dst in zip(old, (*gm, *gs)):
            dst[...] = src[...]

    @pl.when(jnp.logical_not(middle))
    def _():
        share_step(own, near, c, d, mode, weights, accs, gm, gs)

    @pl.when(middle & (k == 0))
    def _():
        s, g = [
            [jnp.concatenate([own_b[t], near_b[t], cd[t], cd[4 + t]], axis=0) for t in (base, base + 1)]
            for base in (0, 2)
        ]
        modes = [jnp.concatenate([m[t, :, :rest] for m in mode], axis=0) for t in range(2)]
        near_modes = [jnp.concatenate([near_mode[2 * i + t] for i in range(4)], axis=0) for t in range(2)]
        q, part = products(s, g, modes, *weights, *accs)
        q_near, part_near = products(s, g, near_modes, *near_weights, *near_accs)
        for t in range(2):
            whole = (part[t] + part_near[t]).astype(BF)
            for i in range(4):
                gm_b[i][t] = q[t][64 * i : 64 * i + 64, :]
                pay[2 * i + t, :, :rest] = q_near[t][64 * i : 64 * i + 64, :]
            gs_own[t] = whole[0:64, :]
            gs_near[t] = whole[64:128, :]
            gs_cd[t] = whole[128:192, :]
            gs_cd[2 + t] = whole[192:256, :]

    @pl.when(middle & (k == 0))
    def _():
        for which, acc in enumerate(near_accs):

            def put(a):
                for i in range(4):
                    pay[2 * i + which, :, rest:] = a[64 * i : 64 * i + 64, :].astype(BF)

            store_factors(info, tmp, acc, put)

    @pl.when(k == steps - 1)
    def _():
        for which, acc in enumerate(accs):

            def put(a):
                d_fac[which] = a

            store_factors(info, tmp, acc, put)


def last(info, own, near, c, d, mode, old, own_b, near_b, cd, near_pay):
    modes, rest = own.shape[2], own_b.shape[2]
    steps = modes // TILE

    def ends(rows):
        return pl.BlockSpec((rows, 64, TILE), lambda k, n: (0, 0, k * (1 - n[16])))

    def middles(rows):
        return pl.BlockSpec((rows, 64, rest), lambda k, n: (0, 0, 0))

    def fixed(rows, at):
        return pl.BlockSpec((rows, 64, 256), lambda k, n: (0, 0, at))

    both = pl.BlockSpec(
        (2, 64, TILE),
        lambda k, n: (0, 0, jnp.where(n[16] == 1, steps, k)),
    )
    square = pl.BlockSpec((2, 256, 256), lambda k, n: (0, 0, 0))
    outs = pl.pallas_call(
        functools.partial(last_body, steps),
        grid_spec=pltpu.PrefetchScalarGridSpec(
            num_scalar_prefetch=1,
            grid=(steps,),
            in_specs=[ends(4)] * 4
            + [both] * 4
            + [fixed(2, mode[0].shape[2] // 256 - 1)] * 4
            + [pl.BlockSpec((2, 64, TILE), lambda k, n: (0, 0, 0))] * 8
            + [middles(4), middles(4), middles(8), middles(8), fixed(8, rest // 256)],
            out_specs=[ends(2)] * 8
            + [square]
            + [middles(2)] * 4
            + [pl.BlockSpec((8, 64, rest + 256), lambda k, n: (0, 0, 0))]
            + [middles(2), middles(2), middles(4)],
            scratch_shapes=[pltpu.VMEM((256, 256), BF)] * 6 + [pltpu.VMEM((256, 256), F32)] * 5,
        ),
        out_shape=[hbm((2, 64, modes), BF)] * 8
        + [hbm((2, 256, 256), F32)]
        + [hbm((2, 64, rest), BF)] * 4
        + [hbm((8, 64, rest + 256), BF)]
        + [hbm((n, 64, rest), BF) for n in (2, 2, 4)],
        input_output_aliases={13 + i: i for i in range(8)},
        compiler_params=pltpu.CompilerParams(vmem_limit_bytes=52 * 1024 * 1024),
        cost_estimate=pl.CostEstimate(
            flops=20 * 256 * 256 * modes, bytes_accessed=10 * 256 * 2 * modes * 2, transcendentals=0
        ),
    )(info, own, near, c, d, *mode, *mode, *old, own_b, near_b, cd, near_pay, near_pay)
    return list(outs[0:4]), outs[4:8], outs[8], list(outs[9:13]), *outs[13:]


def cut(a, x, d, size):
    return lax.dynamic_slice_in_dim(a, ((x + d) % NX) * size, size, axis=2)


def add(a, b):
    return (a.astype(F32) + b.astype(F32)).astype(BF)


def together(*arrays):
    return lax.optimization_barrier(arrays)


def on_device(spectrum, out_grad, in_factor, out_factor, mode_factor):
    scale = float(mode_factor.shape[2] * lax.axis_size("bulk")) ** (-0.5)
    size = mode_factor.shape[2] // NX
    share = SHARE
    place = lax.axis_index("tensor")
    x, z = place % NX, place // NX
    order = jnp.asarray(ORDER, jnp.int32)[z]
    blocks = order[:, None] * NX + (x - jnp.arange(NX, dtype=jnp.int32)[None, :]) % NX
    middle = (z == 1) | (z == 2)
    info = jnp.concatenate([blocks.reshape(16), middle.astype(jnp.int32)[None]])
    turn = lambda a: jnp.transpose(a, (1, 0, 2))

    both = jnp.concatenate([turn(spectrum), turn(out_grad)], axis=0)
    parts = [cut(both, x, d, size) for d in range(NX)]
    parts = [parts[0]] + [send(parts[d], x_shift(d)) for d in range(1, NX)]
    own_a = jnp.concatenate([a[:, :, :share] for a in parts], axis=1)
    own_b = jnp.concatenate([a[:, :, share:] for a in parts], axis=1)

    factors = jnp.stack([in_factor.T, out_factor.T])
    turned = turn(mode_factor)
    mode = [jnp.concatenate([cut(turned, x, d, size), factors], axis=2) for d in range(NX)]

    own_a, mode = together(own_a, mode)
    near_a, c_mid = send(own_a, SWAP), send(own_a, MIDDLE)
    mode = [mode[0]] + [send(mode[i], x_shift(i)) for i in range(1, NX)]
    near_a, c_mid, own_b = together(near_a, c_mid, own_b)
    d_mid, c_end, near_b = send(near_a, MIDDLE), send(c_mid, OUTWARD), send(own_b, INWARD)
    d_mid, c_end, near_b = together(d_mid, c_end, near_b)
    d_end = send(d_mid, OUTWARD)
    near_pay = send(jnp.concatenate([a[:, :, share:] for a in mode], axis=0), INWARD)
    cd_b = send(jnp.concatenate([own_b, near_b], axis=0), MIDDLE)
    *old, d_mid_fac = shared_middle(info, own_a, near_a, c_mid, d_mid, mode)
    near_pay, cd_b, d_end, old, d_mid_fac = together(near_pay, cd_b, d_end, old, d_mid_fac)
    gm_a, (own, near, c, d), d_fac, gm_b, pay, gs_own, gs_near, gs_cd = last(
        info, own_a, near_a, c_end, d_end, mode, old, own_b, near_b, cd_b, near_pay
    )

    from_d = send(d, INWARD)
    pay = send(pay, OUTWARD)
    gm_a[1], gm_a[3] = send(gm_a[1], x_shift(-1)), send(gm_a[3], x_shift(-3))
    from_d, c = together(from_d, c)
    from_c = send(c, INWARD)
    d = send(jnp.concatenate([add(d, from_d), gs_cd[2:4]], axis=2), MIDDLE)
    fac = d_fac.reshape(2, NX, 64, 256)
    mid_fac = d_mid_fac.reshape(2, NX, 64, 256)
    gm_b = [
        jnp.where(
            middle,
            jnp.concatenate([gm_b[i], (fac[:, i] + mid_fac[:, i]).astype(BF)], axis=2),
            jnp.concatenate(
                [pay[2 * i : 2 * i + 2, :, :-256], (fac[:, i] + pay[2 * i : 2 * i + 2, :, -256:]).astype(BF)], axis=2
            ),
        )
        for i in range(NX)
    ]
    gm_b = [gm_b[0]] + [send(gm_b[i], x_shift(-i)) for i in range(1, NX)]
    from_c, d, gm_a = together(from_c, d, gm_a)
    zero = jnp.zeros_like(gs_own)
    near = add(jnp.concatenate([near, jnp.where(middle, gs_near, zero)], axis=2), d)
    c = send(jnp.concatenate([add(c, from_c), gs_cd[0:2]], axis=2), MIDDLE)
    near = send(near, SWAP)
    gm_a[2] = send(gm_a[2], x_shift(2))
    fac = [a[:, :, -256:].astype(F32) for a in gm_b]
    total = (fac[0] + fac[1]) + (fac[2] + fac[3])
    core = lax.axis_index("bulk") % 2
    mine, other = jnp.where(core == 0, total, total[::-1])
    mine = mine + send_bulk(other, lambda i: i ^ 1)
    mine = mine + send_bulk(mine, lambda i: i ^ 4)
    mine = mine + send_bulk(mine, lambda i: i ^ 2)
    c, near, gm_a, gm_b, mine = together(c, near, gm_a, gm_b, mine)
    own = jnp.concatenate([own, jnp.where(middle, gs_own, zero)], axis=2).astype(F32)
    own = (own + c.astype(F32) + near.astype(F32)).astype(BF)
    own = [own[:, 16 * i : 16 * i + 16] for i in range(NX)]
    own = [own[0]] + [send(own[i], x_shift(-i)) for i in range(1, NX)]
    mine = scale * (mine + send_bulk(mine, lambda i: i ^ 8))
    other = send_bulk(mine, lambda i: i ^ 1)
    grad_in = jnp.where(core == 0, mine, other)
    grad_out = jnp.where(core == 0, other, mine)

    def join(parts):
        out = jnp.zeros(parts[0].shape[:2] + (size * NX,), BF)
        for d in range(NX):
            out = lax.dynamic_update_slice_in_dim(out, parts[d], ((x + d) % NX) * size, axis=2)
        return turn(out)

    grad_modes = join([jnp.concatenate([a, b[:, :, :-256]], axis=2) for a, b in zip(gm_a, gm_b)])
    return (join(own), grad_modes, grad_in.T, grad_out.T)


def solution(mesh):
    return jax.shard_map(
        on_device,
        mesh=mesh,
        in_specs=(
            P("tensor", None, "bulk"),
            P("tensor", None, "bulk"),
            P(None, "tensor"),
            P(None, "tensor"),
            P("tensor", None, "bulk"),
        ),
        out_specs=(
            P("tensor", None, "bulk"),
            P("tensor", None, "bulk"),
            P(None, "tensor"),
            P(None, "tensor"),
        ),
        check_vma=False,
    )
```

```python
import functools

import jax
import jax.numpy as jnp
from jax import lax
from jax.experimental import pallas as pl
from jax.experimental.pallas import tpu as pltpu
from jax.sharding import PartitionSpec as P

BF = jnp.bfloat16
F32 = jnp.float32
NX = 4
NZ = 4
ORDER = ((0, 1, 2, 3), (1, 0, 2, 3), (2, 3, 1, 0), (3, 2, 1, 0))


def x_shift(step):
    return [(z * NX + x, z * NX + (x + step) % NX) for z in range(NZ) for x in range(NX)]


def z_moves(pairs):
    return [(a * NX + x, b * NX + x) for a, b in pairs for x in range(NX)]


SWAP = z_moves([(0, 1), (1, 0), (2, 3), (3, 2)])
MIDDLE = z_moves([(1, 2), (2, 1)])
OUTWARD = z_moves([(1, 0), (2, 3)])
INWARD = z_moves([(0, 1), (3, 2)])


def send(a, moves):
    return lax.ppermute(a, "tensor", moves)


def send_bulk(a, move):
    return lax.ppermute(a, "bulk", [(i, move(i)) for i in range(16)])


def y_shift(step):
    return lambda i: (i // 8) * 8 + ((i // 2 % 4 + step) % 4) * 2 + i % 2


def nt_dot(a, b):
    return lax.dot_general(a, b, (((1,), (1,)), ((), ())), preferred_element_type=F32)


def nn_dot(a, b):
    return jnp.dot(a, b, preferred_element_type=F32)


TILE = 256
SHARE = 1792


def hbm(shape, kind):
    return pltpu.HBM(shape, kind)


def load_factors(pieces, info, tmp, acc, rows, cols_in, cols_out):
    for which, row, col in ((0, rows, cols_in), (1, None, cols_out)):
        tmp[...] = jnp.concatenate(pieces(which), axis=0).astype(F32).T
        for i in range(16):
            src = pl.ds(pl.multiple_of(info[i] * 16, 16), 16)
            acc[16 * i : 16 * i + 16, :] = tmp[src, :]
        if row is not None:
            row[...] = acc[...].astype(BF)
        col[...] = acc[...].T.astype(BF)


def store_factors(info, tmp, acc, out):
    for i in range(16):
        dst = pl.ds(pl.multiple_of(info[i] * 16, 16), 16)
        tmp[dst, :] = acc[16 * i : 16 * i + 16, :]
    out(tmp[...].T)


def products(s, g, mode, rows, cols_in, cols_out, acc_in, acc_out):
    m0, m1 = [a.astype(F32) for a in mode]
    u0, u1 = [nn_dot(cols_in[...], a) for a in s]
    v0, v1 = [nn_dot(cols_out[...], a) for a in g]
    w = [(m0 * u0 - m1 * u1).astype(BF), (m0 * u1 + m1 * u0).astype(BF)]
    p = [(v0 * m0 + v1 * m1).astype(BF), (v1 * m0 - v0 * m1).astype(BF)]
    q = [(v0 * u0 + v1 * u1).astype(BF), (v1 * u0 - v0 * u1).astype(BF)]
    acc_in[...] += nt_dot(s[0], p[0]) + nt_dot(s[1], p[1])
    acc_out[...] += nt_dot(g[0], w[0]) + nt_dot(g[1], w[1])
    return q, [nn_dot(rows[...], a) for a in p]


def share_step(own, near, c, d, mode, weights, accs, gm, gs):
    s, g = [
        [jnp.concatenate([own[t], near[t], c[t], d[t]], axis=0) for t in (base, base + 1)]
        for base in (0, 2)
    ]
    modes = [jnp.concatenate([m[t] for m in mode], axis=0) for t in range(2)]
    q, part = products(s, g, modes, *weights, *accs)
    for t in range(2):
        whole = part[t].astype(BF)
        for i in range(4):
            gm[i][t] = q[t][64 * i : 64 * i + 64, :]
            gs[i][t] = whole[64 * i : 64 * i + 64, :]


def shared_body(steps, info, *refs):
    own, near, c, d = refs[0:4]
    mode, fac = refs[4:8], refs[8:12]
    gm, gs, d_fac = refs[12:16], refs[16:20], refs[20]
    weights, tmp, accs = refs[21:24], refs[24], refs[25:27]
    k = pl.program_id(0)
    middle = info[16] == 1

    @pl.when(middle & (k == 0))
    def _():
        load_factors(lambda which: [f[which] for f in fac], info, tmp, accs[0], *weights)
        for acc in accs:
            acc[...] = jnp.zeros_like(acc)

    @pl.when(middle)
    def _():
        share_step(own, near, c, d, mode, weights, accs, gm, gs)

    @pl.when(middle & (k == steps - 1))
    def _():
        for which, acc in enumerate(accs):

            def put(a):
                d_fac[which] = a

            store_factors(info, tmp, acc, put)


def shared_middle(info, own, near, c, d, mode):
    modes = own.shape[2]
    steps = modes // TILE

    def tiles(rows):
        return pl.BlockSpec((rows, 64, TILE), lambda k, n: (0, 0, k * n[16]))

    last = mode[0].shape[2] // 256 - 1
    fac = pl.BlockSpec((2, 64, 256), lambda k, n: (0, 0, last))
    square = pl.BlockSpec((2, 256, 256), lambda k, n: (0, 0, 0))
    return pl.pallas_call(
        functools.partial(shared_body, steps),
        grid_spec=pltpu.PrefetchScalarGridSpec(
            num_scalar_prefetch=1,
            grid=(steps,),
            in_specs=[tiles(4)] * 4 + [tiles(2)] * 4 + [fac] * 4,
            out_specs=[tiles(2)] * 8 + [square],
            scratch_shapes=[pltpu.VMEM((256, 256), BF)] * 3 + [pltpu.VMEM((256, 256), F32)] * 3,
        ),
        out_shape=[hbm((2, 64, modes), BF)] * 8 + [hbm((2, 256, 256), F32)],
        compiler_params=pltpu.CompilerParams(vmem_limit_bytes=32 * 1024 * 1024),
        cost_estimate=pl.CostEstimate(
            flops=20 * 256 * 256 * modes, bytes_accessed=10 * 256 * 2 * modes * 2, transcendentals=0
        ),
    )(info, own, near, c, d, *mode, *mode)


def last_body(steps, info, *refs):
    own, near, c, d = refs[0:4]
    mode, fac, old = refs[4:8], refs[8:12], refs[12:20]
    own_b, near_b, cd, near_mode, near_fac = refs[20:25]
    gm, gs, d_fac = refs[25:29], refs[29:33], refs[33]
    gm_b, pay, gs_own, gs_near, gs_cd = refs[34:38], *refs[38:42]
    weights, near_weights, tmp = refs[42:45], refs[45:48], refs[48]
    accs, near_accs = refs[49:51], refs[51:53]
    k = pl.program_id(0)
    middle = info[16] == 1
    rest = pay.shape[2] - 256

    @pl.when(k == 0)
    def _():
        load_factors(lambda which: [f[which] for f in fac], info, tmp, accs[0], *weights)
        for acc in accs:
            acc[...] = jnp.zeros_like(acc)

    @pl.when(middle & (k == 0))
    def _():
        load_factors(
            lambda which: [near_fac[2 * i + which] for i in range(4)], info, tmp, near_accs[0], *near_weights
        )
        for acc in near_accs:
            acc[...] = jnp.zeros_like(acc)
        for src, dst in zip(old, (*gm, *gs)):
            dst[...] = src[...]

    @pl.when(jnp.logical_not(middle))
    def _():
        share_step(own, near, c, d, mode, weights, accs, gm, gs)

    @pl.when(middle & (k < rest // TILE))
    def _():
        s, g = [
            [jnp.concatenate([own_b[t], near_b[t], cd[t], cd[4 + t]], axis=0) for t in (base, base + 1)]
            for base in (0, 2)
        ]
        modes = [jnp.concatenate([m[t] for m in mode], axis=0) for t in range(2)]
        near_modes = [jnp.concatenate([near_mode[2 * i + t] for i in range(4)], axis=0) for t in range(2)]
        q, part = products(s, g, modes, *weights, *accs)
        q_near, part_near = products(s, g, near_modes, *near_weights, *near_accs)
        here = pl.ds(pl.multiple_of(k * TILE, TILE), TILE)
        for t in range(2):
            whole = (part[t] + part_near[t]).astype(BF)
            for i in range(4):
                gm_b[i][t] = q[t][64 * i : 64 * i + 64, :]
                pay[2 * i + t, :, here] = q_near[t][64 * i : 64 * i + 64, :]
            gs_own[t] = whole[0:64, :]
            gs_near[t] = whole[64:128, :]
            gs_cd[t] = whole[128:192, :]
            gs_cd[2 + t] = whole[192:256, :]

    @pl.when(middle & (k == rest // TILE - 1))
    def _():
        for which, acc in enumerate(near_accs):

            def put(a):
                for i in range(4):
                    pay[2 * i + which, :, rest:] = a[64 * i : 64 * i + 64, :].astype(BF)

            store_factors(info, tmp, acc, put)

    @pl.when(k == steps - 1)
    def _():
        for which, acc in enumerate(accs):

            def put(a):
                d_fac[which] = a

            store_factors(info, tmp, acc, put)


def last(info, own, near, c, d, mode, old, own_b, near_b, cd, near_pay):
    modes, rest = own.shape[2], own_b.shape[2]
    steps, rest_steps = modes // TILE, rest // TILE

    def ends(rows):
        return pl.BlockSpec((rows, 64, TILE), lambda k, n: (0, 0, k * (1 - n[16])))

    def middles(rows):
        return pl.BlockSpec((rows, 64, TILE), lambda k, n: (0, 0, jnp.minimum(k, rest_steps - 1) * n[16]))

    def fixed(rows, at):
        return pl.BlockSpec((rows, 64, 256), lambda k, n: (0, 0, at))

    both = pl.BlockSpec(
        (2, 64, TILE),
        lambda k, n: (0, 0, jnp.where(n[16] == 1, steps + jnp.minimum(k, rest_steps - 1), k)),
    )
    square = pl.BlockSpec((2, 256, 256), lambda k, n: (0, 0, 0))
    outs = pl.pallas_call(
        functools.partial(last_body, steps),
        grid_spec=pltpu.PrefetchScalarGridSpec(
            num_scalar_prefetch=1,
            grid=(steps,),
            in_specs=[ends(4)] * 4
            + [both] * 4
            + [fixed(2, mode[0].shape[2] // 256 - 1)] * 4
            + [fixed(2, 0)] * 8
            + [middles(4), middles(4), middles(8), middles(8), fixed(8, rest // 256)],
            out_specs=[ends(2)] * 8
            + [square]
            + [middles(2)] * 4
            + [pl.BlockSpec((8, 64, rest + 256), lambda k, n: (0, 0, 0))]
            + [middles(2), middles(2), middles(4)],
            scratch_shapes=[pltpu.VMEM((256, 256), BF)] * 6 + [pltpu.VMEM((256, 256), F32)] * 5,
        ),
        out_shape=[hbm((2, 64, modes), BF)] * 8
        + [hbm((2, 256, 256), F32)]
        + [hbm((2, 64, rest), BF)] * 4
        + [hbm((8, 64, rest + 256), BF)]
        + [hbm((n, 64, rest), BF) for n in (2, 2, 4)],
        input_output_aliases={13 + i: i for i in range(8)},
        compiler_params=pltpu.CompilerParams(vmem_limit_bytes=40 * 1024 * 1024),
        cost_estimate=pl.CostEstimate(
            flops=20 * 256 * 256 * modes, bytes_accessed=10 * 256 * 2 * modes * 2, transcendentals=0
        ),
    )(info, own, near, c, d, *mode, *mode, *old, own_b, near_b, cd, near_pay, near_pay)
    return list(outs[0:4]), outs[4:8], outs[8], list(outs[9:13]), *outs[13:]


def cut(a, x, d, size):
    return lax.dynamic_slice_in_dim(a, ((x + d) % NX) * size, size, axis=2)


def add(a, b):
    return (a.astype(F32) + b.astype(F32)).astype(BF)


def together(*arrays):
    return lax.optimization_barrier(arrays)


def on_device(spectrum, out_grad, in_factor, out_factor, mode_factor):
    scale = float(mode_factor.shape[2] * lax.axis_size("bulk")) ** (-0.5)
    size = mode_factor.shape[2] // NX
    share = SHARE
    place = lax.axis_index("tensor")
    x, z = place % NX, place // NX
    order = jnp.asarray(ORDER, jnp.int32)[z]
    blocks = order[:, None] * NX + (x - jnp.arange(NX, dtype=jnp.int32)[None, :]) % NX
    middle = (z == 1) | (z == 2)
    info = jnp.concatenate([blocks.reshape(16), middle.astype(jnp.int32)[None]])
    turn = lambda a: jnp.transpose(a, (1, 0, 2))

    both = jnp.concatenate([turn(spectrum), turn(out_grad)], axis=0)
    parts = [cut(both, x, d, size) for d in range(NX)]
    parts = [parts[0]] + [send(parts[d], x_shift(d)) for d in range(1, NX)]
    own_a = jnp.concatenate([a[:, :, :share] for a in parts], axis=1)
    own_b = jnp.concatenate([a[:, :, share:] for a in parts], axis=1)

    factors = jnp.stack([in_factor.T, out_factor.T])
    turned = turn(mode_factor)
    mode = [jnp.concatenate([cut(turned, x, d, size), factors], axis=2) for d in range(NX)]

    own_a, mode = together(own_a, mode)
    near_a, c_mid = send(own_a, SWAP), send(own_a, MIDDLE)
    mode = [mode[0]] + [send(mode[i], x_shift(i)) for i in range(1, NX)]
    near_a, c_mid, own_b = together(near_a, c_mid, own_b)
    d_mid, c_end, near_b = send(near_a, MIDDLE), send(c_mid, OUTWARD), send(own_b, INWARD)
    d_mid, c_end, near_b = together(d_mid, c_end, near_b)
    d_end = send(d_mid, OUTWARD)
    near_pay = send(jnp.concatenate([a[:, :, share:] for a in mode], axis=0), INWARD)
    cd_b = send(jnp.concatenate([own_b, near_b], axis=0), MIDDLE)
    *old, d_mid_fac = shared_middle(info, own_a, near_a, c_mid, d_mid, mode)
    near_pay, cd_b, d_end, old, d_mid_fac = together(near_pay, cd_b, d_end, old, d_mid_fac)
    gm_a, (own, near, c, d), d_fac, gm_b, pay, gs_own, gs_near, gs_cd = last(
        info, own_a, near_a, c_end, d_end, mode, old, own_b, near_b, cd_b, near_pay
    )

    from_d = send(d, INWARD)
    pay = send(pay, OUTWARD)
    gm_a[1], gm_a[3] = send(gm_a[1], x_shift(-1)), send(gm_a[3], x_shift(-3))
    from_d, c = together(from_d, c)
    from_c = send(c, INWARD)
    d = send(jnp.concatenate([add(d, from_d), gs_cd[2:4]], axis=2), MIDDLE)
    fac = d_fac.reshape(2, NX, 64, 256)
    mid_fac = d_mid_fac.reshape(2, NX, 64, 256)
    gm_b = [
        jnp.where(
            middle,
            jnp.concatenate([gm_b[i], (fac[:, i] + mid_fac[:, i]).astype(BF)], axis=2),
            jnp.concatenate(
                [pay[2 * i : 2 * i + 2, :, :-256], (fac[:, i] + pay[2 * i : 2 * i + 2, :, -256:]).astype(BF)], axis=2
            ),
        )
        for i in range(NX)
    ]
    gm_b = [gm_b[0]] + [send(gm_b[i], x_shift(-i)) for i in range(1, NX)]
    from_c, d, gm_a = together(from_c, d, gm_a)
    zero = jnp.zeros_like(gs_own)
    near = add(jnp.concatenate([near, jnp.where(middle, gs_near, zero)], axis=2), d)
    c = send(jnp.concatenate([add(c, from_c), gs_cd[0:2]], axis=2), MIDDLE)
    near = send(near, SWAP)
    gm_a[2] = send(gm_a[2], x_shift(2))
    fac = [a[:, :, -256:].astype(F32) for a in gm_b]
    total = (fac[0] + fac[1]) + (fac[2] + fac[3])
    core = lax.axis_index("bulk") % 2
    mine, other = jnp.where(core == 0, total, total[::-1])
    mine = mine + send_bulk(other, lambda i: i ^ 1)
    mine = mine + send_bulk(mine, lambda i: i ^ 4)
    mine = mine + send_bulk(mine, lambda i: i ^ 2)
    c, near, gm_a, gm_b, mine = together(c, near, gm_a, gm_b, mine)
    own = jnp.concatenate([own, jnp.where(middle, gs_own, zero)], axis=2).astype(F32)
    own = (own + c.astype(F32) + near.astype(F32)).astype(BF)
    own = [own[:, 16 * i : 16 * i + 16] for i in range(NX)]
    own = [own[0]] + [send(own[i], x_shift(-i)) for i in range(1, NX)]
    mine = scale * (mine + send_bulk(mine, lambda i: i ^ 8))
    other = send_bulk(mine, lambda i: i ^ 1)
    grad_in = jnp.where(core == 0, mine, other)
    grad_out = jnp.where(core == 0, other, mine)

    def join(parts):
        out = jnp.zeros(parts[0].shape[:2] + (size * NX,), BF)
        for d in range(NX):
            out = lax.dynamic_update_slice_in_dim(out, parts[d], ((x + d) % NX) * size, axis=2)
        return turn(out)

    grad_modes = join([jnp.concatenate([a, b[:, :, :-256]], axis=2) for a, b in zip(gm_a, gm_b)])
    return (join(own), grad_modes, grad_in.T, grad_out.T)


def solution(mesh):
    return jax.shard_map(
        on_device,
        mesh=mesh,
        in_specs=(
            P("tensor", None, "bulk"),
            P("tensor", None, "bulk"),
            P(None, "tensor"),
            P(None, "tensor"),
            P("tensor", None, "bulk"),
        ),
        out_specs=(
            P("tensor", None, "bulk"),
            P("tensor", None, "bulk"),
            P(None, "tensor"),
            P(None, "tensor"),
        ),
        check_vma=False,
    )
```
